32 devices in a mesh: grp: 2 (over y), rows: 8 (over z, x), heads: 2 (over core).
Axes of the slice: x: 2, y: 2, z: 4, core: 2. Of those that a mesh axis runs over, the one named last changes fastest.
Arguments:
- pre_state: bfloat16 [32, 128, 64, 128], P(('grp', 'rows'), 'heads'), parts along dimension 0, may hold values from -6 to 6
- pre_conv: bfloat16 [32, 3, 4, 2304], P(('grp', 'rows'), None, 'heads'), parts along dimension 0, may hold values from -6 to 6
- resident_state: bfloat16 [64, 128, 64, 128], P(('grp', 'rows'), 'heads'), parts along dimension 0, may hold values from -6 to 6
- resident_conv: bfloat16 [64, 3, 4, 2304], P(('grp', 'rows'), None, 'heads'), parts along dimension 0, may hold values from -6 to 6
- source_slot: int32 [16], P(('grp', 'rows')), parts along dimension 0, may hold values from 0 to 15, as said below
- target_row: int32 [16], P(('grp', 'rows')), parts along dimension 0, may hold values from 0 to 31, as said below
- conv_input: bfloat16 [4, 64, 4, 2304], P(None, ('grp', 'rows'), 'heads'), parts along dimension 1, may hold values from -6 to 6
- delta_raw: bfloat16 [4, 64, 128], P(None, ('grp', 'rows'), 'heads'), parts along dimension 1, may hold values from -4 to 4
- gate_input: bfloat16 [4, 64, 8192], P(None, ('grp', 'rows'), 'heads'), parts along dimension 1, may hold values from -6 to 6
- active: int32 [4, 64], P(None, ('grp', 'rows')), parts along dimension 1, may hold values 0 or 1
- conv_weight: float32 [4, 4, 2304], P(None, 'heads'), may hold values from -3 to 3
- conv_bias: float32 [4, 2304], P('heads'), may hold values from -0.5 to 0.5
- delta_bias: float32 [128], P('heads'), may hold values from -2 to 0.5
- decay_log: float32 [128], P('heads'), may hold values from -4 to 0.5
- skip_gain: float32 [128], P('heads'), may hold values from 0.5 to 2
- norm_gain: float32 [8192], P('heads'), may hold values from 0.5 to 1.5
Outputs:
- layer_output: bfloat16 [4, 64, 8192], P(None, ('grp', 'rows'), 'heads'), parts along dimension 1
- final_state: bfloat16 [64, 128, 64, 128], P(('grp', 'rows'), 'heads'), parts along dimension 0
- final_conv: bfloat16 [64, 3, 4, 2304], P(('grp', 'rows'), None, 'heads'), parts along dimension 0
The draws below stay inside these ranges and needn't reach their ends.
There are 2 independent parts, one for each index of `grp`. The reference program is written for one: setup_inputs(seed, part) draws one part's arguments, and reference() takes and returns one part's arrays. A program takes and returns all parts, laid end to end along the dimension named above; an argument that names none is the same for every part. Nothing has to cross between parts.
Inputs may be any that keep to these rules, and one draw needn't show every extreme that they name: `source_slot`: 8 distinct slots. `target_row`: 8 distinct rows; the 4 rows of one index of rows receive at most 4 prompts, and in every draw some index receives 4.
All inputs are finite; a program needn't handle non-finite values. No bound on the sum of `active` on one device may be relied on, other than what follows from the above.
Results may differ from the reference program's by a relative error of at most 0.001.
Values may be sent and summed in bfloat16 or wider, within the bound.
A program may use at most 64 MiB of HBM per device.

```python
import jax
import jax.numpy as jnp
from jax import lax

H = 128
G = 4
P_SIZE = 64
N = 128
K = 4
STEPS = 4
ROW_DEV = 4
ROWS = 32
PSLOTS = 16
PROMPTS = 8
INNER = 8192
CG = 2304


def pick_subset(key, total_count, pick_count, forced):
    key_one, key_two = jax.random.split(key)
    rank_values = jax.random.permutation(key_one, total_count).astype(jnp.int32)
    scores = jnp.where(forced, rank_values - total_count, rank_values)
    ordering = jnp.argsort(scores, stable=True)
    chosen = ordering[:pick_count]
    return chosen[jax.random.permutation(key_two, pick_count)].astype(jnp.int32)


def draw_source_slot(key, part):
    key = jax.random.fold_in(key, 11)
    places = jnp.arange(PSLOTS, dtype=jnp.int32)
    forced = (places == 0) | (places == PSLOTS - 1)
    return pick_subset(key, PSLOTS, PROMPTS, forced)


def draw_target_row(key, part):
    key = jax.random.fold_in(key, 23)
    key_device, key_pick = jax.random.split(key)
    places = jnp.arange(ROWS, dtype=jnp.int32)
    device = jax.random.randint(key_device, (), 0, ROWS // ROW_DEV, dtype=jnp.int32)
    forced = (places // ROW_DEV == device) | (places == 0) | (places == ROWS - 1)
    return pick_subset(key_pick, ROWS, PROMPTS, forced)


def with_ends(entries, rng, low, largest):
    longest = entries.shape.index(max(entries.shape))
    spots = []
    for shift in (0, 1):
        where = [jax.random.randint(jax.random.fold_in(rng, axis), (), 0, length) for axis, length in enumerate(entries.shape)]
        where[longest] = (where[longest] + shift) % entries.shape[longest]
        spots.append(tuple(where))
    return entries.at[spots[0]].set(low).at[spots[1]].set(largest)


def block_scale(rng, dims, shards, least, top_value):
    def one(dim, parts):
        steps = jax.random.uniform(jax.random.fold_in(jax.random.fold_in(rng, 6), dim), (parts,), jnp.float32, least / len(shards), top_value / len(shards))
        return jnp.repeat(jnp.exp(steps), dims[dim] // parts).reshape((-1,) + (1,) * (len(dims) - dim - 1))

    factor_of = one(*shards[0])
    for cut in shards[1:]:
        factor_of = factor_of * one(*cut)
    return factor_of


def bell_draw(stream_key, extent, spread, bound, cuts=(), kind=jnp.bfloat16):
    entries = spread * jax.random.normal(stream_key, extent, jnp.float32)
    if cuts:
        entries = entries * block_scale(stream_key, extent, cuts, -0.22, 0.18)
    return jnp.clip(entries, -bound, bound).astype(kind)


def setup_inputs(seed: int = 0, part: int = 0) -> dict:
    streams_of = jax.random.split(jax.random.key(seed), 17)
    part_keys = jax.random.split(jax.random.fold_in(streams_of[16], part), 17)
    return {
        "pre_state": bell_draw(part_keys[0], (PSLOTS, H, P_SIZE, N), 1.0, 6.0, ((0, 8), (1, 2))),
        "pre_conv": bell_draw(part_keys[1], (PSLOTS, K - 1, G, CG), 1.0, 6.0, ((0, 8), (2, 2))),
        "resident_state": bell_draw(part_keys[2], (ROWS, H, P_SIZE, N), 1.0, 6.0, ((0, 8), (1, 2))),
        "resident_conv": bell_draw(part_keys[3], (ROWS, K - 1, G, CG), 1.0, 6.0, ((0, 8), (2, 2))),
        "source_slot": draw_source_slot(jax.random.fold_in(jax.random.fold_in(streams_of[16], part), 71), part),
        "target_row": draw_target_row(jax.random.fold_in(jax.random.fold_in(streams_of[16], part), 71), part),
        "conv_input": bell_draw(part_keys[6], (STEPS, ROWS, G, CG), 1.0, 6.0, ((1, 8), (2, 2))),
        "delta_raw": bell_draw(part_keys[7], (STEPS, ROWS, H), 1.0, 4.0, ((1, 8), (2, 2))),
        "gate_input": bell_draw(part_keys[8], (STEPS, ROWS, INNER), 1.0, 6.0, ((1, 8), (2, 2))),
        "active": with_ends((jax.random.randint(part_keys[9], (STEPS, ROWS), 0, 4) < 3).astype(jnp.int32), jax.random.fold_in(part_keys[9], 1), 0, 1),
        "conv_weight": bell_draw(streams_of[10], (K, G, CG), K ** -0.5, 3.0, ((1, 2),), jnp.float32),
        "conv_bias": jnp.clip(jax.random.uniform(streams_of[11], (G, CG), jnp.float32, -0.5, 0.5) * block_scale(streams_of[11], (G, CG), ((0, 2),), -0.4, 0.0), -0.5, 0.5),
        "delta_bias": jnp.clip(-2.0 + 2.5 * jax.random.uniform(streams_of[12], (H,), jnp.float32) ** block_scale(streams_of[12], (H,), ((0, 2),), -0.2, 0.2), -2.0, 0.5),
        "decay_log": jnp.clip(-4.0 + 4.5 * jax.random.uniform(streams_of[13], (H,), jnp.float32) ** block_scale(streams_of[13], (H,), ((0, 2),), -0.2, 0.2), -4.0, 0.5),
        "skip_gain": jnp.clip(0.5 + 1.5 * jax.random.uniform(streams_of[14], (H,), jnp.float32) ** block_scale(streams_of[14], (H,), ((0, 2),), -0.2, 0.2), 0.5, 2.0),
        "norm_gain": jnp.clip(1.0 + 0.1 * jax.random.normal(streams_of[15], (INNER,), jnp.float32), 0.5, 1.5),
    }


def decode_block(states, conv_rows, conv_input, delta_raw, gate_input, active, conv_weight, conv_bias, delta_bias, decay_log, skip_gain, norm_gain):
    steps_total = conv_input.shape[0]
    row_count, head_count, head_size, state_size = states.shape
    group_count = conv_rows.shape[2]
    per_group = head_count // group_count
    value_width = per_group * head_size
    carried = states.astype(jnp.float32)
    history = conv_rows.astype(jnp.float32)
    decay_rates = jnp.exp(decay_log)
    results = []
    for step_index in range(steps_total):
        window = jnp.concatenate([history, conv_input[step_index][:, None].astype(jnp.float32)], axis=1)
        convolved = jax.nn.silu(lax.optimization_barrier(jnp.sum(window * conv_weight[None], axis=1)) + conv_bias[None])
        inputs = convolved[..., :value_width].reshape(row_count, head_count, head_size)
        write_heads = jnp.repeat(convolved[..., value_width:value_width + state_size], per_group, axis=1)
        read_heads = jnp.repeat(convolved[..., value_width + state_size:], per_group, axis=1)
        step_size = jax.nn.softplus(delta_raw[step_index].astype(jnp.float32) + delta_bias[None])
        retention = jnp.exp(-decay_rates[None] * step_size)
        updated = retention[:, :, None, None] * carried + (step_size[:, :, None] * inputs)[..., None] * write_heads[:, :, None, :]
        readout = lax.optimization_barrier(jnp.sum(updated * read_heads[:, :, None, :], axis=-1)) + skip_gain[None, :, None] * inputs
        gated_out = readout.reshape(row_count, head_count * head_size) * jax.nn.silu(gate_input[step_index].astype(jnp.float32))
        grouped = gated_out.reshape(row_count, group_count, value_width)
        inverse_rms = lax.rsqrt(lax.optimization_barrier(jnp.mean(grouped * grouped, axis=-1, keepdims=True)) + 1e-05)
        normed = (grouped * inverse_rms).reshape(row_count, head_count * head_size) * norm_gain[None]
        live_rows = active[step_index] == 1
        carried = jnp.where(live_rows[:, None, None, None], updated, carried)
        history = jnp.where(live_rows[:, None, None, None], window[:, 1:], history)
        results.append(jnp.where(live_rows[:, None], normed, jnp.zeros_like(normed)).astype(jnp.bfloat16))
    return (jnp.stack(results), carried.astype(jnp.bfloat16), history.astype(jnp.bfloat16))

def reference(pre_state, pre_conv, resident_state, resident_conv, source_slot, target_row, conv_input, delta_raw, gate_input, active, conv_weight, conv_bias, delta_bias, decay_log, skip_gain, norm_gain):
    start_state = resident_state.at[target_row].set(pre_state[source_slot])
    start_conv = resident_conv.at[target_row].set(pre_conv[source_slot])
    blocks = ROWS // ROW_DEV

    def split_rows(array):
        return array.reshape((blocks, ROW_DEV) + array.shape[1:])

    def split_steps(array):
        return jnp.swapaxes(array.reshape((array.shape[0], blocks, ROW_DEV) + array.shape[2:]), 0, 1)

    def decode_one(pieces):
        return decode_block(pieces[0], pieces[1], pieces[2], pieces[3], pieces[4], pieces[5], conv_weight, conv_bias, delta_bias, decay_log, skip_gain, norm_gain)
    outputs, final_state, final_conv = lax.map(decode_one, (split_rows(start_state), split_rows(start_conv), split_steps(conv_input), split_steps(delta_raw), split_steps(gate_input), split_steps(active)))
    layer_output = jnp.swapaxes(outputs, 0, 1).reshape(STEPS, ROWS, INNER)
    return (layer_output, final_state.reshape(resident_state.shape), final_conv.reshape(resident_conv.shape))
```

```python
import functools

import jax
import jax.numpy as jnp
from jax import lax
from jax.experimental import pallas as pl
from jax.experimental.pallas import tpu as pltpu
from jax.sharding import PartitionSpec as P

F32 = jnp.float32
BF16 = jnp.bfloat16


def split_two(values):
    high = lax.reduce_precision(values, exponent_bits=8, mantissa_bits=7)
    return high.astype(BF16), (values - high).astype(BF16)


def prepare(
    history,
    conv_input,
    delta_raw,
    gate_input,
    active,
    conv_weight,
    conv_bias,
    delta_bias,
    decay_log,
    skip_gain,
    norm_gain,
    state_size,
    head_size,
):
    steps, rows = conv_input.shape[:2]
    groups = conv_bias.shape[0]
    heads = delta_bias.shape[0]
    per_group = heads // groups
    width = per_group * head_size
    live = active == 1
    history = [history[:, k].astype(F32) for k in range(history.shape[1])]
    decay_rates = jnp.exp(decay_log)
    xs, bs, cs, log_as, deltas = [], [], [], [], []
    for t in range(steps):
        window = history + [conv_input[t].astype(F32)]
        total = window[0] * conv_weight[0][None]
        for k in range(1, len(window)):
            total = total + window[k] * conv_weight[k][None]
        u = jax.nn.silu(total + conv_bias[None])
        xs.append(u[..., :width].reshape(rows, heads, head_size))
        bs.append(u[..., width : width + state_size])
        cs.append(u[..., width + state_size :])
        delta = jax.nn.softplus(delta_raw[t].astype(F32) + delta_bias[None])
        deltas.append(delta)
        log_as.append(-decay_rates[None] * delta)
        keep = live[t][:, None, None]
        history = [jnp.where(keep, window[k + 1], history[k]) for k in range(len(history))]
    final_conv = jnp.stack(history, axis=1).astype(BF16)
    x = jnp.stack(xs, axis=1)
    b = jnp.stack(bs, axis=1)
    c = jnp.stack(cs, axis=1)
    delta = jnp.stack(deltas, axis=1)
    log_a = jnp.stack(log_as, axis=1)
    live_rt = live.T[:, :, None]
    live_log = jnp.where(live_rt, log_a, 0.0)
    live_delta = jnp.where(live_rt, delta, 0.0)
    bc = jnp.sum(b[:, None] * c[:, :, None], axis=-1)
    bc = jnp.repeat(bc, per_group, axis=-1)
    intra, through = [], []
    for t in range(steps):
        part = (skip_gain[None] + delta[:, t] * bc[:, t, t])[..., None] * x[:, t]
        reach = log_a[:, t]
        for s in range(t - 1, -1, -1):
            weight = jnp.exp(reach) * live_delta[:, s] * bc[:, t, s]
            part = part + weight[..., None] * x[:, s]
            reach = reach + live_log[:, s]
        intra.append(part)
        through.append(jnp.exp(reach))
    gate = jax.nn.silu(gate_input.astype(F32)).swapaxes(0, 1)
    y0 = jnp.stack(intra, axis=1).reshape(gate.shape) * gate
    scale = jnp.repeat(jnp.stack(through, axis=1), head_size, axis=-1) * gate
    tails = []
    reach = jnp.zeros_like(live_log[:, 0])
    for s in range(steps - 1, -1, -1):
        tails.append(jnp.exp(reach) * live_delta[:, s])
        reach = reach + live_log[:, s]
    tail = jnp.stack(tails[::-1], axis=1)
    keep_all = jnp.broadcast_to(jnp.exp(reach)[..., None], (rows, heads, state_size))
    coef = (tail[..., None] * x).reshape(rows, steps, heads * head_size)
    coef_hi, coef_lo = split_two(coef)
    b_hi, b_lo = split_two(b.swapaxes(1, 2))
    c_hi, c_lo = split_two(c.swapaxes(1, 2))
    left = jnp.concatenate([coef_hi, coef_hi, coef_lo, jnp.zeros_like(coef_hi)], axis=1)
    right = jnp.concatenate([b_hi, b_lo, b_hi, jnp.zeros_like(b_hi)], axis=2)
    reads = jnp.concatenate([c_hi, c_lo, jnp.zeros_like(c_hi), jnp.zeros_like(c_lo)], axis=2)
    gain = jnp.where(live.T[:, :, None], norm_gain[None, None], 0.0)
    return final_conv, scale, y0, gain, keep_all, left, right, reads


def update_kernel(
    steps, flags, came, resident, scale, y0, gain, keep, left, right, reads, out, final, rows_out
):
    r = pl.program_id(0)
    g = pl.program_id(1)
    per_group, head_size, state_size = resident.shape[1:]
    width = per_group * head_size
    arrived = flags[r] == 1

    def run(source):
        s0 = source.reshape(width, state_size)
        read = lax.dot_general(
            reads[0, 0], s0, (((1,), (1,)), ((), ())), preferred_element_type=F32
        )
        q = read[:steps] + read[steps : 2 * steps]
        v = scale[0] * q + y0[0]
        mean = jnp.mean(v * v, axis=-1, keepdims=True)
        normed = v * lax.rsqrt(mean + 1e-05) * gain[0]
        for t in range(steps):
            rows_out[t, pl.ds(r, 1), pl.ds(pl.multiple_of(g * width, 128), width)] = normed[
                t : t + 1
            ]
        update = lax.dot_general(
            left[0], right[0, 0], (((0,), (0,)), ((), ())), preferred_element_type=F32
        )
        for h in range(per_group):
            span = slice(h * head_size, (h + 1) * head_size)
            final[0, h] = (
                keep[0, h : h + 1] * s0[span].astype(F32) + update[span]
            ).astype(BF16)

    @pl.when(arrived)
    def _():
        run(came[...])

    @pl.when(jnp.logical_not(arrived))
    def _():
        run(resident[...])

    @pl.when((r == pl.num_programs(0) - 1) & (g == pl.num_programs(1) - 1))
    def _():
        out[...] = rows_out[...].astype(BF16)


def update_rows(flags, came, resident, scale, y0, gain, keep, left, right, reads):
    rows, heads, head_size, state_size = resident.shape
    groups = reads.shape[1]
    steps = scale.shape[1]
    per_group = heads // groups
    width = per_group * head_size
    pieces, _, piece_heads = came.shape[:3]
    wide = lambda lines: pl.BlockSpec((1, lines, width), lambda r, g, f: (r, 0, g))
    small = pl.BlockSpec((1, 1, 4 * steps, state_size), lambda r, g, f: (r, g, 0, 0))
    state_spec = pl.BlockSpec(
        (1, per_group, head_size, state_size), lambda r, g, f: (r, g, 0, 0)
    )
    return pl.pallas_call(
        functools.partial(update_kernel, steps),
        grid_spec=pltpu.PrefetchScalarGridSpec(
            num_scalar_prefetch=1,
            grid=(rows, groups),
            in_specs=[
                pl.BlockSpec(
                    (pieces // groups, 1, piece_heads, head_size, state_size),
                    lambda r, g, f: (g, r, 0, 0, 0),
                ),
                state_spec,
                wide(steps),
                wide(steps),
                wide(steps),
                pl.BlockSpec((1, per_group, state_size), lambda r, g, f: (r, g, 0)),
                wide(4 * steps),
                small,
                small,
            ],
            out_specs=[
                pl.BlockSpec((steps, rows, heads * head_size), lambda r, g, f: (0, 0, 0)),
                state_spec,
            ],
            scratch_shapes=[pltpu.VMEM((steps, rows, heads * head_size), F32)],
        ),
        out_shape=[
            jax.ShapeDtypeStruct((steps, rows, heads * head_size), BF16),
            jax.ShapeDtypeStruct(resident.shape, BF16),
        ],
        compiler_params=pltpu.CompilerParams(vmem_limit_bytes=40 * 1024 * 1024),
    )(flags, came, resident, scale, y0, gain, keep, left, right, reads)


def per_device(
    pre_state,
    pre_conv,
    resident_state,
    resident_conv,
    source_slot,
    target_row,
    conv_input,
    delta_raw,
    gate_input,
    active,
    conv_weight,
    conv_bias,
    delta_bias,
    decay_log,
    skip_gain,
    norm_gain,
):
    devices = lax.axis_size("rows")
    slots, heads, head_size, state_size = pre_state.shape
    rows = resident_state.shape[0]
    all_source = lax.all_gather(source_slot, "rows", axis=0, tiled=True)
    all_target = lax.all_gather(target_row, "rows", axis=0, tiled=True)
    matches = all_target[None, :] == jnp.arange(devices * rows, dtype=jnp.int32)[:, None]
    arrival = jnp.any(matches, axis=1)
    slot_for_row = jnp.sum(jnp.where(matches, all_source[None, :], 0), axis=1)
    first = lax.axis_index("rows") * rows
    own_arrival = lax.dynamic_slice_in_dim(arrival, first, rows)
    own_slot = lax.dynamic_slice_in_dim(slot_for_row, first, rows)

    piece_heads = heads // devices
    pieces = pre_state.reshape(slots, devices, piece_heads, head_size, state_size)
    held = lax.all_to_all(pieces, "rows", split_axis=1, concat_axis=0, tiled=True)
    held = held.reshape(devices * slots, piece_heads, head_size, state_size)
    outgoing = held[slot_for_row].reshape(devices, rows, piece_heads, head_size, state_size)
    came = lax.all_to_all(outgoing, "rows", split_axis=0, concat_axis=0, tiled=True)

    all_conv = lax.all_gather(pre_conv, "rows", axis=0, tiled=True)
    start_conv = jnp.where(own_arrival[:, None, None, None], all_conv[own_slot], resident_conv)
    final_conv, *small = prepare(
        start_conv,
        conv_input,
        delta_raw,
        gate_input,
        active,
        conv_weight,
        conv_bias,
        delta_bias,
        decay_log,
        skip_gain,
        norm_gain,
        state_size,
        head_size,
    )
    layer_output, final_state = update_rows(
        own_arrival.astype(jnp.int32), came, resident_state, *small
    )
    return layer_output, final_state, final_conv


def solution(mesh):
    in_specs = (
        P(("grp", "rows"), "heads", None, None),
        P(("grp", "rows"), None, "heads", None),
        P(("grp", "rows"), "heads", None, None),
        P(("grp", "rows"), None, "heads", None),
        P(("grp", "rows")),
        P(("grp", "rows")),
        P(None, ("grp", "rows"), "heads", None),
        P(None, ("grp", "rows"), "heads"),
        P(None, ("grp", "rows"), "heads"),
        P(None, ("grp", "rows")),
        P(None, "heads", None),
        P("heads", None),
        P("heads"),
        P("heads"),
        P("heads"),
        P("heads"),
    )
    out_specs = (
        P(None, ("grp", "rows"), "heads"),
        P(("grp", "rows"), "heads", None, None),
        P(("grp", "rows"), None, "heads", None),
    )
    return jax.shard_map(
        per_device, mesh=mesh, in_specs=in_specs, out_specs=out_specs, check_vma=False
    )
```

```python
import functools

import jax
import jax.numpy as jnp
from jax import lax
from jax.experimental import pallas as pl
from jax.experimental.pallas import tpu as pltpu
from jax.sharding import PartitionSpec as P

F32 = jnp.float32
BF16 = jnp.bfloat16


def split_two(values):
    high = lax.reduce_precision(values, exponent_bits=8, mantissa_bits=7)
    return high.astype(BF16), (values - high).astype(BF16)


def prepare(
    history,
    conv_input,
    delta_raw,
    gate_input,
    active,
    conv_weight,
    conv_bias,
    delta_bias,
    decay_log,
    skip_gain,
    norm_gain,
    state_size,
    head_size,
):
    steps, rows = conv_input.shape[:2]
    groups = conv_bias.shape[0]
    heads = delta_bias.shape[0]
    per_group = heads // groups
    width = per_group * head_size
    live = active == 1
    history = [history[:, k].astype(F32) for k in range(history.shape[1])]
    decay_rates = jnp.exp(decay_log)
    xs, bs, cs, log_as, deltas = [], [], [], [], []
    for t in range(steps):
        window = history + [conv_input[t].astype(F32)]
        total = window[0] * conv_weight[0][None]
        for k in range(1, len(window)):
            total = total + window[k] * conv_weight[k][None]
        u = jax.nn.silu(total + conv_bias[None])
        xs.append(u[..., :width].reshape(rows, heads, head_size))
        bs.append(u[..., width : width + state_size])
        cs.append(u[..., width + state_size :])
        delta = jax.nn.softplus(delta_raw[t].astype(F32) + delta_bias[None])
        deltas.append(delta)
        log_as.append(-decay_rates[None] * delta)
        keep = live[t][:, None, None]
        history = [jnp.where(keep, window[k + 1], history[k]) for k in range(len(history))]
    final_conv = jnp.stack(history, axis=1).astype(BF16)
    x = jnp.stack(xs, axis=1)
    b = jnp.stack(bs, axis=1)
    c = jnp.stack(cs, axis=1)
    delta = jnp.stack(deltas, axis=1)
    log_a = jnp.stack(log_as, axis=1)
    live_rt = live.T[:, :, None]
    live_log = jnp.where(live_rt, log_a, 0.0)
    live_delta = jnp.where(live_rt, delta, 0.0)
    bc = jnp.sum(b[:, None] * c[:, :, None], axis=-1)
    bc = jnp.repeat(bc, per_group, axis=-1)
    intra, through = [], []
    for t in range(steps):
        part = (skip_gain[None] + delta[:, t] * bc[:, t, t])[..., None] * x[:, t]
        reach = log_a[:, t]
        for s in range(t - 1, -1, -1):
            weight = jnp.exp(reach) * live_delta[:, s] * bc[:, t, s]
            part = part + weight[..., None] * x[:, s]
            reach = reach + live_log[:, s]
        intra.append(part)
        through.append(jnp.exp(reach))
    gate = jax.nn.silu(gate_input.astype(F32)).swapaxes(0, 1)
    y0 = jnp.stack(intra, axis=1).reshape(gate.shape) * gate
    scale = jnp.repeat(jnp.stack(through, axis=1), head_size, axis=-1) * gate
    tails = []
    reach = jnp.zeros_like(live_log[:, 0])
    for s in range(steps - 1, -1, -1):
        tails.append(jnp.exp(reach) * live_delta[:, s])
        reach = reach + live_log[:, s]
    tail = jnp.stack(tails[::-1], axis=1)
    keep_all = jnp.broadcast_to(jnp.exp(reach)[..., None], (rows, heads, state_size))
    coef = (tail[..., None] * x).reshape(rows, steps, heads * head_size)
    coef_hi, coef_lo = split_two(coef)
    b_hi, b_lo = split_two(b.swapaxes(1, 2))
    c_hi, c_lo = split_two(c.swapaxes(1, 2))
    left = jnp.concatenate([coef_hi, coef_hi, coef_lo, jnp.zeros_like(coef_hi)], axis=1)
    right = jnp.concatenate([b_hi, b_lo, b_hi, jnp.zeros_like(b_hi)], axis=2)
    reads = jnp.concatenate([c_hi, c_lo, jnp.zeros_like(c_hi), jnp.zeros_like(c_lo)], axis=2)
    gain = jnp.where(live.T[:, :, None], norm_gain[None, None], 0.0)
    return final_conv, scale, y0, gain, keep_all, left, right, reads


def update_kernel(
    steps, flags, came, resident, scale, y0, gain, keep, left, right, reads, out, final, rows_out
):
    r = pl.program_id(0)
    g = pl.program_id(1)
    per_group, head_size, state_size = resident.shape[1:]
    width = per_group * head_size
    arrived = flags[r] == 1

    def run(source):
        s0 = source.reshape(width, state_size)
        read = lax.dot_general(
            reads[0, 0], s0, (((1,), (1,)), ((), ())), preferred_element_type=F32
        )
        q = read[:steps] + read[steps : 2 * steps]
        v = scale[0] * q + y0[0]
        mean = jnp.mean(v * v, axis=-1, keepdims=True)
        normed = v * lax.rsqrt(mean + 1e-05) * gain[0]
        for t in range(steps):
            rows_out[t, pl.ds(r, 1), pl.ds(pl.multiple_of(g * width, 128), width)] = normed[
                t : t + 1
            ]
        update = lax.dot_general(
            left[0], right[0, 0], (((0,), (0,)), ((), ())), preferred_element_type=F32
        )
        for h in range(per_group):
            span = slice(h * head_size, (h + 1) * head_size)
            final[0, h] = (
                keep[0, h : h + 1] * s0[span].astype(F32) + update[span]
            ).astype(BF16)

    @pl.when(arrived)
    def _():
        run(came[...])

    @pl.when(jnp.logical_not(arrived))
    def _():
        run(resident[...])

    @pl.when((r == pl.num_programs(0) - 1) & (g == pl.num_programs(1) - 1))
    def _():
        out[...] = rows_out[...].astype(BF16)


def update_rows(flags, came, resident, scale, y0, gain, keep, left, right, reads):
    rows, heads, head_size, state_size = resident.shape
    groups = reads.shape[1]
    steps = scale.shape[1]
    per_group = heads // groups
    width = per_group * head_size
    pieces, _, piece_heads = came.shape[:3]
    wide = lambda lines: pl.BlockSpec((1, lines, width), lambda r, g, f: (r, 0, g))
    small = pl.BlockSpec((1, 1, 4 * steps, state_size), lambda r, g, f: (r, g, 0, 0))
    state_spec = pl.BlockSpec(
        (1, per_group, head_size, state_size), lambda r, g, f: (r, g, 0, 0)
    )
    return pl.pallas_call(
        functools.partial(update_kernel, steps),
        grid_spec=pltpu.PrefetchScalarGridSpec(
            num_scalar_prefetch=1,
            grid=(rows, groups),
            in_specs=[
                pl.BlockSpec(
                    (pieces // groups, 1, piece_heads, head_size, state_size),
                    lambda r, g, f: (g, r, 0, 0, 0),
                ),
                state_spec,
                wide(steps),
                wide(steps),
                wide(steps),
                pl.BlockSpec((1, per_group, state_size), lambda r, g, f: (r, g, 0)),
                wide(4 * steps),
                small,
                small,
            ],
            out_specs=[
                pl.BlockSpec((steps, rows, heads * head_size), lambda r, g, f: (0, 0, 0)),
                state_spec,
            ],
            scratch_shapes=[pltpu.VMEM((steps, rows, heads * head_size), F32)],
        ),
        out_shape=[
            jax.ShapeDtypeStruct((steps, rows, heads * head_size), BF16),
            jax.ShapeDtypeStruct(resident.shape, BF16),
        ],
        compiler_params=pltpu.CompilerParams(vmem_limit_bytes=40 * 1024 * 1024),
    )(flags, came, resident, scale, y0, gain, keep, left, right, reads)


def route_kernel(
    inner, slots, rows, pre, pre_conv, info, came, came_conv, infos,
    held, held_conv, out, out_conv, table,
    local_sem, spread_send, spread_recv, line_send, line_recv, hop_send, hop_recv,
    *buffers,
):
    devices = lax.axis_size("rows")
    outer = devices // inner
    half = len(buffers) // 2
    lines = list(zip(buffers[:half], buffers[half:]))
    prompts = buffers[0].shape[0]
    me = lax.axis_index("rows")
    z = me // inner
    x = me % inner

    barrier = pltpu.get_barrier_semaphore()
    for j in range(1, devices):
        pl.semaphore_signal(
            barrier, inc=1, device_id={"rows": lax.rem(me + j, devices)},
            device_id_type=pl.DeviceIdType.MESH,
        )
    pl.semaphore_wait(barrier, devices - 1)

    def remote(src, dst, send, recv, peer):
        return pltpu.make_async_remote_copy(
            src_ref=src, dst_ref=dst, send_sem=send, recv_sem=recv,
            device_id={"rows": peer}, device_id_type=pl.DeviceIdType.MESH,
        )

    mine = pl.ds(me * slots, slots)
    spread = []
    for j in range(1, devices):
        peer = lax.rem(me + j, devices)
        for k, (src, dst) in enumerate((
            (info.at[0], infos.at[me]),
            (pre_conv.at[:, peer], held_conv.at[mine]),
            (pre.at[:, peer], held.at[mine]),
        )):
            spread.append(remote(src, dst, spread_send.at[k, j], spread_recv.at[k, j], peer))
    for copy in spread:
        copy.start()
    own = [
        pltpu.make_async_copy(info.at[0], infos.at[me], local_sem.at[0]),
        pltpu.make_async_copy(pre_conv.at[:, me], held_conv.at[mine], local_sem.at[1]),
        pltpu.make_async_copy(pre.at[:, me], held.at[mine], local_sem.at[2]),
    ]
    for copy in own:
        copy.start()
    for copy in own:
        copy.wait()
    for copy in spread:
        copy.wait_recv()
    to_table = pltpu.make_async_copy(infos, table, local_sem.at[3])
    to_table.start()
    to_table.wait()

    def pick(q, carry):
        slot = table[q, 0, 0]
        lines[0][0][q] = held[slot]
        lines[0][1][q] = held_conv[slot]
        return carry

    lax.fori_loop(0, prompts, pick, 0)

    def prompt_of(row):
        def look(q, found):
            return jnp.where(table[q, 0, 1] == row, q, found)

        return lax.fori_loop(0, prompts, look, 0)

    wanted = [
        [prompt_of((z * inner + lax.rem(x + j, inner)) * rows + k) for k in range(rows)]
        for j in range(inner)
    ]

    def hop(block, j):
        peer = z * inner + lax.rem(x + j, inner)
        piece = block * inner + x
        return [
            remote(out.at[block, j - 1], came.at[piece], hop_send.at[0, block, j - 1],
                   hop_recv.at[0, block, j - 1], peer),
            remote(out_conv.at[block, j - 1], came_conv.at[piece], hop_send.at[1, block, j - 1],
                   hop_recv.at[1, block, j - 1], peer),
        ]

    def deliver(block, line, line_conv):
        for j in range(1, inner):
            for k in range(rows):
                out[block, j - 1, k] = line[wanted[j][k]]
                out_conv[block, j - 1, k] = line_conv[wanted[j][k]]
            for copy in hop(block, j):
                copy.start()
        for k in range(rows):
            came[block * inner + x, k] = line[wanted[0][k]]
            came_conv[block * inner + x, k] = line_conv[wanted[0][k]]

    def landed(s, way):
        return lines[0] if s < 0 else lines[1 + (way + 1) // 2 * (outer - 1) + s]

    def step_copies(s, way):
        side = (way + 1) // 2
        return [
            remote(src, dst, line_send.at[k, side, s], line_recv.at[k, side, s], me + way * inner)
            for k, (src, dst) in enumerate(zip(landed(s - 1, way), landed(s, way)))
        ]

    def sends(s, way):
        ok = (z - way * s >= 0) & (z - way * s < outer) & (z + way >= 0) & (z + way < outer)
        return ok

    def receives(s, way):
        origin = z - way - way * s
        return (origin >= 0) & (origin < outer)

    def arrivals(s, way):
        side = (way + 1) // 2
        return [
            remote(dst, dst, line_send.at[k, side, s], line_recv.at[k, side, s], me - way * inner)
            for k, dst in enumerate(landed(s, way))
        ]

    for s in range(outer - 1):
        for way in (1, -1):
            @pl.when(sends(s, way))
            def _():
                for copy in step_copies(s, way):
                    copy.start()

        if s == 0:
            deliver(z, *lines[0])
        else:
            for way in (1, -1):
                @pl.when(receives(s - 1, way))
                def _():
                    deliver(z - way * s, *landed(s - 1, way))

        for way in (1, -1):
            @pl.when(receives(s, way))
            def _():
                for copy in arrivals(s, way):
                    copy.wait_recv()

    for way in (1, -1):
        @pl.when(receives(outer - 2, way))
        def _():
            deliver(z - way * (outer - 1), *landed(outer - 2, way))

    for copy in spread:
        copy.wait_send()
    for s in range(outer - 1):
        for way in (1, -1):
            @pl.when(sends(s, way))
            def _():
                for copy in step_copies(s, way):
                    copy.wait_send()

    for block in range(outer):
        for j in range(1, inner):
            source = lax.rem(x + inner - j, inner)
            piece = block * inner + source
            for copy in hop(block, j):
                copy.wait_send()
            remote(out.at[block, j - 1], came.at[piece], hop_send.at[0, block, j - 1],
                   hop_recv.at[0, block, j - 1], z * inner + source).wait_recv()
            remote(out_conv.at[block, j - 1], came_conv.at[piece], hop_send.at[1, block, j - 1],
                   hop_recv.at[1, block, j - 1], z * inner + source).wait_recv()


def route(pre, pre_conv, info, rows):
    slots, devices, piece_heads, head_size, state_size = pre.shape
    lines = pre_conv.shape[2]
    inner = 4 if devices % 16 == 0 else 2
    outer = devices // inner
    prompts = devices
    state = (piece_heads, head_size, state_size)
    conv = (lines, 128)
    vmem = pl.BlockSpec(memory_space=pltpu.VMEM)
    dma = pltpu.SemaphoreType.DMA
    return pl.pallas_call(
        functools.partial(route_kernel, inner, slots, rows),
        in_specs=[pl.BlockSpec(memory_space=pl.ANY), vmem, vmem],
        out_specs=[vmem, vmem, vmem],
        out_shape=[
            jax.ShapeDtypeStruct((devices, rows) + state, BF16),
            jax.ShapeDtypeStruct((devices, rows) + conv, BF16),
            jax.ShapeDtypeStruct((devices, 1, 128), jnp.int32),
        ],
        scratch_shapes=[
            pltpu.VMEM((devices * slots,) + state, BF16),
            pltpu.VMEM((devices * slots,) + conv, BF16),
            pltpu.VMEM((outer, inner - 1, rows) + state, BF16),
            pltpu.VMEM((outer, inner - 1, rows) + conv, BF16),
            pltpu.SMEM((devices, 1, 128), jnp.int32),
            dma((4,)),
            dma((3, devices)),
            dma((3, devices)),
            dma((2, 2, outer - 1)),
            dma((2, 2, outer - 1)),
            dma((2, outer, inner - 1)),
            dma((2, outer, inner - 1)),
        ]
        + [pltpu.VMEM((prompts,) + state, BF16)] * (2 * outer - 1)
        + [pltpu.VMEM((prompts,) + conv, BF16)] * (2 * outer - 1),
        compiler_params=pltpu.CompilerParams(
            collective_id=0, has_side_effects=True, vmem_limit_bytes=56 * 1024 * 1024
        ),
    )(pre, pre_conv, info)


def per_device(
    pre_state,
    pre_conv,
    resident_state,
    resident_conv,
    source_slot,
    target_row,
    conv_input,
    delta_raw,
    gate_input,
    active,
    conv_weight,
    conv_bias,
    delta_bias,
    decay_log,
    skip_gain,
    norm_gain,
):
    devices = lax.axis_size("rows")
    slots, heads, head_size, state_size = pre_state.shape
    rows = resident_state.shape[0]
    piece_heads = heads // devices
    pieces = pre_state.reshape(slots, devices, piece_heads, head_size, state_size)
    conv_size = pre_conv[0].size // devices
    lines = -(-conv_size // (16 * 128)) * 16
    conv_pieces = jnp.pad(
        pre_conv.reshape(slots, devices, conv_size), ((0, 0), (0, 0), (0, lines * 128 - conv_size))
    ).reshape(slots, devices, lines, 128)
    info = jnp.pad(jnp.stack([source_slot, target_row], axis=1), ((0, 0), (0, 126)))
    came, came_conv, infos = route(pieces, conv_pieces, info.reshape(1, 1, 128), rows)

    own_rows = lax.axis_index("rows") * rows + jnp.arange(rows, dtype=jnp.int32)
    own_arrival = jnp.any(infos[:, 0, 1][None, :] == own_rows[:, None], axis=1)
    arrived_conv = came_conv.reshape(devices, rows, lines * 128)[..., :conv_size]
    arrived_conv = arrived_conv.swapaxes(0, 1).reshape(resident_conv.shape)
    start_conv = jnp.where(own_arrival[:, None, None, None], arrived_conv, resident_conv)
    final_conv, *small = prepare(
        start_conv,
        conv_input,
        delta_raw,
        gate_input,
        active,
        conv_weight,
        conv_bias,
        delta_bias,
        decay_log,
        skip_gain,
        norm_gain,
        state_size,
        head_size,
    )
    layer_output, final_state = update_rows(
        own_arrival.astype(jnp.int32), came, resident_state, *small
    )
    return layer_output, final_state, final_conv


def solution(mesh):
    in_specs = (
        P(("grp", "rows"), "heads", None, None),
        P(("grp", "rows"), None, "heads", None),
        P(("grp", "rows"), "heads", None, None),
        P(("grp", "rows"), None, "heads", None),
        P(("grp", "rows")),
        P(("grp", "rows")),
        P(None, ("grp", "rows"), "heads", None),
        P(None, ("grp", "rows"), "heads"),
        P(None, ("grp", "rows"), "heads"),
        P(None, ("grp", "rows")),
        P(None, "heads", None),
        P("heads", None),
        P("heads"),
        P("heads"),
        P("heads"),
        P("heads"),
    )
    out_specs = (
        P(None, ("grp", "rows"), "heads"),
        P(("grp", "rows"), "heads", None, None),
        P(("grp", "rows"), None, "heads", None),
    )
    return jax.shard_map(
        per_device, mesh=mesh, in_specs=in_specs, out_specs=out_specs, check_vma=False
    )
```

```python
import functools

import jax
import jax.numpy as jnp
from jax import lax
from jax.experimental import pallas as pl
from jax.experimental.pallas import tpu as pltpu
from jax.sharding import PartitionSpec as P

F32 = jnp.float32
BF16 = jnp.bfloat16
CHUNKS = 2


def split_two(values):
    high = lax.reduce_precision(values, exponent_bits=8, mantissa_bits=7)
    return high.astype(BF16), (values - high).astype(BF16)


def prepare(
    history,
    conv_input,
    delta_raw,
    gate_input,
    active,
    conv_weight,
    conv_bias,
    delta_bias,
    decay_log,
    skip_gain,
    norm_gain,
    state_size,
    head_size,
):
    steps, rows = conv_input.shape[:2]
    groups = conv_bias.shape[0]
    heads = delta_bias.shape[0]
    per_group = heads // groups
    width = per_group * head_size
    live = active == 1
    history = [history[:, k].astype(F32) for k in range(history.shape[1])]
    decay_rates = jnp.exp(decay_log)
    xs, bs, cs, log_as, deltas = [], [], [], [], []
    for t in range(steps):
        window = history + [conv_input[t].astype(F32)]
        total = window[0] * conv_weight[0][None]
        for k in range(1, len(window)):
            total = total + window[k] * conv_weight[k][None]
        u = jax.nn.silu(total + conv_bias[None])
        xs.append(u[..., :width].reshape(rows, heads, head_size))
        bs.append(u[..., width : width + state_size])
        cs.append(u[..., width + state_size :])
        delta = jax.nn.softplus(delta_raw[t].astype(F32) + delta_bias[None])
        deltas.append(delta)
        log_as.append(-decay_rates[None] * delta)
        keep = live[t][:, None, None]
        history = [jnp.where(keep, window[k + 1], history[k]) for k in range(len(history))]
    final_conv = jnp.stack(history, axis=1).astype(BF16)
    x = jnp.stack(xs, axis=1)
    b = jnp.stack(bs, axis=1)
    c = jnp.stack(cs, axis=1)
    delta = jnp.stack(deltas, axis=1)
    log_a = jnp.stack(log_as, axis=1)
    live_rt = live.T[:, :, None]
    live_log = jnp.where(live_rt, log_a, 0.0)
    live_delta = jnp.where(live_rt, delta, 0.0)
    bc = jnp.sum(b[:, None] * c[:, :, None], axis=-1)
    bc = jnp.repeat(bc, per_group, axis=-1)
    intra, through = [], []
    for t in range(steps):
        part = (skip_gain[None] + delta[:, t] * bc[:, t, t])[..., None] * x[:, t]
        reach = log_a[:, t]
        for s in range(t - 1, -1, -1):
            weight = jnp.exp(reach) * live_delta[:, s] * bc[:, t, s]
            part = part + weight[..., None] * x[:, s]
            reach = reach + live_log[:, s]
        intra.append(part)
        through.append(jnp.exp(reach))
    gate = jax.nn.silu(gate_input.astype(F32)).swapaxes(0, 1)
    y0 = jnp.stack(intra, axis=1).reshape(gate.shape) * gate
    scale = jnp.repeat(jnp.stack(through, axis=1), head_size, axis=-1) * gate
    tails = []
    reach = jnp.zeros_like(live_log[:, 0])
    for s in range(steps - 1, -1, -1):
        tails.append(jnp.exp(reach) * live_delta[:, s])
        reach = reach + live_log[:, s]
    tail = jnp.stack(tails[::-1], axis=1)
    keep_all = jnp.broadcast_to(jnp.exp(reach)[..., None], (rows, heads, state_size))
    coef = (tail[..., None] * x).reshape(rows, steps, heads * head_size)
    coef_hi, coef_lo = split_two(coef)
    b_hi, b_lo = split_two(b.swapaxes(1, 2))
    c_hi, c_lo = split_two(c.swapaxes(1, 2))
    left = jnp.concatenate([coef_hi, coef_hi, coef_lo, jnp.zeros_like(coef_hi)], axis=1)
    right = jnp.concatenate([b_hi, b_lo, b_hi, jnp.zeros_like(b_hi)], axis=2)
    reads = jnp.concatenate([c_hi, c_lo, jnp.zeros_like(c_hi), jnp.zeros_like(c_lo)], axis=2)
    gain = jnp.where(live.T[:, :, None], norm_gain[None, None], 0.0)
    return final_conv, scale, y0, gain, keep_all, left, right, reads


def update_kernel(
    steps, flags, came, resident, scale, y0, gain, keep, left, right, reads, out, final, rows_out
):
    r = pl.program_id(0)
    g = pl.program_id(1)
    per_group, head_size, state_size = resident.shape[1:]
    width = per_group * head_size
    arrived = flags[r] == 1

    def run(source):
        s0 = source.reshape(width, state_size)
        read = lax.dot_general(
            reads[0, 0], s0, (((1,), (1,)), ((), ())), preferred_element_type=F32
        )
        q = read[:steps] + read[steps : 2 * steps]
        v = scale[0] * q + y0[0]
        mean = jnp.mean(v * v, axis=-1, keepdims=True)
        normed = v * lax.rsqrt(mean + 1e-05) * gain[0]
        for t in range(steps):
            rows_out[t, pl.ds(r, 1), pl.ds(pl.multiple_of(g * width, 128), width)] = normed[
                t : t + 1
            ]
        update = lax.dot_general(
            left[0], right[0, 0], (((0,), (0,)), ((), ())), preferred_element_type=F32
        )
        for h in range(per_group):
            span = slice(h * head_size, (h + 1) * head_size)
            final[0, h] = (
                keep[0, h : h + 1] * s0[span].astype(F32) + update[span]
            ).astype(BF16)

    @pl.when(arrived)
    def _():
        run(came[...])

    @pl.when(jnp.logical_not(arrived))
    def _():
        run(resident[...])

    @pl.when((r == pl.num_programs(0) - 1) & (g == pl.num_programs(1) - 1))
    def _():
        out[...] = rows_out[...].astype(BF16)


def update_rows(flags, came, resident, scale, y0, gain, keep, left, right, reads):
    rows, heads, head_size, state_size = resident.shape
    groups = reads.shape[1]
    steps = scale.shape[1]
    per_group = heads // groups
    width = per_group * head_size
    pieces, _, piece_heads = came.shape[:3]
    wide = lambda lines: pl.BlockSpec((1, lines, width), lambda r, g, f: (r, 0, g))
    small = pl.BlockSpec((1, 1, 4 * steps, state_size), lambda r, g, f: (r, g, 0, 0))
    state_spec = pl.BlockSpec(
        (1, per_group, head_size, state_size), lambda r, g, f: (r, g, 0, 0)
    )
    return pl.pallas_call(
        functools.partial(update_kernel, steps),
        grid_spec=pltpu.PrefetchScalarGridSpec(
            num_scalar_prefetch=1,
            grid=(rows, groups),
            in_specs=[
                pl.BlockSpec(
                    (pieces // groups, 1, piece_heads, head_size, state_size),
                    lambda r, g, f: (g, r, 0, 0, 0),
                ),
                state_spec,
                wide(steps),
                wide(steps),
                wide(steps),
                pl.BlockSpec((1, per_group, state_size), lambda r, g, f: (r, g, 0)),
                wide(4 * steps),
                small,
                small,
            ],
            out_specs=[
                pl.BlockSpec((steps, rows, heads * head_size), lambda r, g, f: (0, 0, 0)),
                state_spec,
            ],
            scratch_shapes=[pltpu.VMEM((steps, rows, heads * head_size), F32)],
        ),
        out_shape=[
            jax.ShapeDtypeStruct((steps, rows, heads * head_size), BF16),
            jax.ShapeDtypeStruct(resident.shape, BF16),
        ],
        compiler_params=pltpu.CompilerParams(vmem_limit_bytes=56 * 1024 * 1024),
    )(flags, came, resident, scale, y0, gain, keep, left, right, reads)


def route_kernel(
    inner, slots, rows, chunks, pre, pre_conv, info, came, came_conv, infos, table,
    local_sem, spread_send, spread_recv, line_send, line_recv, hop_send, hop_recv,
    *buffers,
):
    devices = lax.axis_size("rows")
    outer = devices // inner
    part = pre.shape[2] // chunks
    count = 2 * outer + 1
    state_bufs = [buffers[c * count : (c + 1) * count] for c in range(chunks)]
    conv_bufs = buffers[chunks * count :]
    prompts = conv_bufs[2].shape[0]
    me = lax.axis_index("rows")
    z = me // inner
    x = me % inner
    mine = pl.ds(me * slots, slots)

    barrier = pltpu.get_barrier_semaphore()
    for j in range(1, devices):
        pl.semaphore_signal(
            barrier, inc=1, device_id={"rows": lax.rem(me + j, devices)},
            device_id_type=pl.DeviceIdType.MESH,
        )
    pl.semaphore_wait(barrier, devices - 1)

    def remote(src, dst, send, recv, peer):
        return pltpu.make_async_remote_copy(
            src_ref=src, dst_ref=dst, send_sem=send, recv_sem=recv,
            device_id={"rows": peer}, device_id_type=pl.DeviceIdType.MESH,
        )

    def heads_of(c):
        return pl.ds(c * part, part)

    def sets(c):
        return [state_bufs[c]] + ([conv_bufs] if c == 0 else [])

    def pairs(c, peer):
        result = [(pre.at[:, peer, heads_of(c)], state_bufs[c][0].at[mine])]
        if c == 0:
            result.append((pre_conv.at[:, peer], conv_bufs[0].at[mine]))
            result.append((info.at[0], infos.at[me]))
        return result

    def spread(c):
        copies = []
        for j in sorted(range(1, devices), key=lambda j: (abs(j - devices // 2), j)):
            peer = lax.rem(me + j, devices)
            for k, (src, dst) in reversed(list(enumerate(pairs(c, peer)))):
                copies.append(
                    remote(src, dst, spread_send.at[k, c, j], spread_recv.at[k, c, j], peer)
                )
        return copies

    def keep(c):
        return [
            pltpu.make_async_copy(src, dst, local_sem.at[k, c])
            for k, (src, dst) in enumerate(pairs(c, me))
        ]

    def start_spread(c):
        for copy in spread(c) + keep(c):
            copy.start()

    start_spread(0)
    for copy in keep(0):
        copy.wait()
    for copy in spread(0):
        copy.wait_recv()
    if chunks > 1:
        start_spread(1)
    to_table = pltpu.make_async_copy(infos, table, local_sem.at[3, 0])
    to_table.start()
    to_table.wait()

    def prompt_of(row):
        def look(q, found):
            return jnp.where(table[q, 0, 1] == row, q, found)

        return lax.fori_loop(0, prompts, look, 0)

    wanted = [
        [prompt_of((z * inner + lax.rem(x + j, inner)) * rows + k) for k in range(rows)]
        for j in range(inner)
    ]

    def target(k, c, piece):
        return came.at[piece, :, heads_of(c)] if k == 0 else came_conv.at[piece]

    def hop(c, block, j, piece, peer):
        return [
            remote(bufs[1].at[block, j - 1], target(k, c, piece), hop_send.at[k, c, block, j - 1],
                   hop_recv.at[k, c, block, j - 1], peer)
            for k, bufs in enumerate(sets(c))
        ]

    def landed(s, way):
        return 2 if s < 0 else 3 + (way + 1) // 2 * (outer - 1) + s

    def deliver(c, block, s, way):
        piece = block * inner + x
        for j in range(1, inner):
            for k in range(rows):
                for bufs in sets(c):
                    bufs[1][block, j - 1, k] = bufs[landed(s, way)][wanted[j][k]]
            for copy in hop(c, block, j, piece, z * inner + lax.rem(x + j, inner)):
                copy.start()
        for k in range(rows):
            came[piece, k, heads_of(c)] = state_bufs[c][landed(s, way)][wanted[0][k]]
            if c == 0:
                came_conv[piece, k] = conv_bufs[landed(s, way)][wanted[0][k]]

    def step_copies(c, s, way):
        side = (way + 1) // 2
        return [
            remote(bufs[landed(s - 1, way)], bufs[landed(s, way)], line_send.at[k, c, side, s],
                   line_recv.at[k, c, side, s], me + way * inner)
            for k, bufs in enumerate(sets(c))
        ]

    def arrivals(c, s, way):
        side = (way + 1) // 2
        return [
            remote(bufs[landed(s, way)], bufs[landed(s, way)], line_send.at[k, c, side, s],
                   line_recv.at[k, c, side, s], me - way * inner)
            for k, bufs in enumerate(sets(c))
        ]

    def sends(s, way):
        return (z - way * s >= 0) & (z - way * s < outer) & (z + way >= 0) & (z + way < outer)

    def receives(s, way):
        origin = z - way - way * s
        return (origin >= 0) & (origin < outer)

    for c in range(chunks):
        if c > 0:
            for copy in keep(c):
                copy.wait()
            for copy in spread(c):
                copy.wait_recv()
            if c + 1 < chunks:
                start_spread(c + 1)

        def pick(q, carry):
            slot = table[q, 0, 0]
            for bufs in sets(c):
                bufs[2][q] = bufs[0][slot]
            return carry

        lax.fori_loop(0, prompts, pick, 0)

        for s in range(outer - 1):
            for way in (1, -1):
                @pl.when(sends(s, way))
                def _():
                    for copy in step_copies(c, s, way):
                        copy.start()

            if s == 0:
                deliver(c, z, -1, 1)
            else:
                for way in (1, -1):
                    @pl.when(receives(s - 1, way))
                    def _():
                        deliver(c, z - way * s, s - 1, way)

            for way in (1, -1):
                @pl.when(receives(s, way))
                def _():
                    for copy in arrivals(c, s, way):
                        copy.wait_recv()

        for way in (1, -1):
            @pl.when(receives(outer - 2, way))
            def _():
                deliver(c, z - way * (outer - 1), outer - 2, way)

    for c in range(chunks):
        for copy in spread(c):
            copy.wait_send()
        for s in range(outer - 1):
            for way in (1, -1):
                @pl.when(sends(s, way))
                def _():
                    for copy in step_copies(c, s, way):
                        copy.wait_send()
        for block in range(outer):
            for j in range(1, inner):
                source = lax.rem(x + inner - j, inner)
                for copy in hop(c, block, j, block * inner + source, z * inner + source):
                    copy.wait_send()
                    copy.wait_recv()


def route(pre, pre_conv, info, rows):
    slots, devices, piece_heads, head_size, state_size = pre.shape
    lines = pre_conv.shape[2]
    inner = 4 if devices % 16 == 0 else 2
    outer = devices // inner
    prompts = devices
    chunks = min(CHUNKS, piece_heads)
    state = (piece_heads, head_size, state_size)
    part = (piece_heads // chunks, head_size, state_size)

    def buffers(item):
        return [
            pltpu.VMEM((devices * slots,) + item, BF16),
            pltpu.VMEM((outer, inner - 1, rows) + item, BF16),
        ] + [pltpu.VMEM((prompts,) + item, BF16)] * (2 * outer - 1)

    conv = (lines, 128)
    vmem = pl.BlockSpec(memory_space=pltpu.VMEM)
    dma = pltpu.SemaphoreType.DMA
    return pl.pallas_call(
        functools.partial(route_kernel, inner, slots, rows, chunks),
        in_specs=[pl.BlockSpec(memory_space=pl.ANY), vmem, vmem],
        out_specs=[vmem, vmem, vmem],
        out_shape=[
            jax.ShapeDtypeStruct((devices, rows) + state, BF16),
            jax.ShapeDtypeStruct((devices, rows) + conv, BF16),
            jax.ShapeDtypeStruct((devices, 1, 128), jnp.int32),
        ],
        scratch_shapes=[
            pltpu.SMEM((devices, 1, 128), jnp.int32),
            dma((4, chunks)),
            dma((3, chunks, devices)),
            dma((3, chunks, devices)),
            dma((2, chunks, 2, outer - 1)),
            dma((2, chunks, 2, outer - 1)),
            dma((2, chunks, outer, inner - 1)),
            dma((2, chunks, outer, inner - 1)),
        ]
        + buffers(part) * chunks
        + buffers(conv),
        compiler_params=pltpu.CompilerParams(
            collective_id=0, has_side_effects=True, vmem_limit_bytes=56 * 1024 * 1024
        ),
    )(pre, pre_conv, info)


def per_device(
    pre_state,
    pre_conv,
    resident_state,
    resident_conv,
    source_slot,
    target_row,
    conv_input,
    delta_raw,
    gate_input,
    active,
    conv_weight,
    conv_bias,
    delta_bias,
    decay_log,
    skip_gain,
    norm_gain,
):
    devices = lax.axis_size("rows")
    slots, heads, head_size, state_size = pre_state.shape
    rows = resident_state.shape[0]
    piece_heads = heads // devices
    pieces = pre_state.reshape(slots, devices, piece_heads, head_size, state_size)
    conv_size = pre_conv[0].size // devices
    lines = -(-conv_size // (16 * 128)) * 16
    conv_pieces = jnp.pad(
        pre_conv.reshape(slots, devices, conv_size), ((0, 0), (0, 0), (0, lines * 128 - conv_size))
    ).reshape(slots, devices, lines, 128)
    info = jnp.pad(jnp.stack([source_slot, target_row], axis=1), ((0, 0), (0, 126)))
    came, came_conv, infos = route(pieces, conv_pieces, info.reshape(1, 1, 128), rows)

    own_rows = lax.axis_index("rows") * rows + jnp.arange(rows, dtype=jnp.int32)
    own_arrival = jnp.any(infos[:, 0, 1][None, :] == own_rows[:, None], axis=1)
    arrived_conv = came_conv.reshape(devices, rows, lines * 128)[..., :conv_size]
    arrived_conv = arrived_conv.swapaxes(0, 1).reshape(resident_conv.shape)
    start_conv = jnp.where(own_arrival[:, None, None, None], arrived_conv, resident_conv)
    final_conv, *small = prepare(
        start_conv,
        conv_input,
        delta_raw,
        gate_input,
        active,
        conv_weight,
        conv_bias,
        delta_bias,
        decay_log,
        skip_gain,
        norm_gain,
        state_size,
        head_size,
    )
    layer_output, final_state = update_rows(
        own_arrival.astype(jnp.int32), came, resident_state, *small
    )
    return layer_output, final_state, final_conv


def solution(mesh):
    in_specs = (
        P(("grp", "rows"), "heads", None, None),
        P(("grp", "rows"), None, "heads", None),
        P(("grp", "rows"), "heads", None, None),
        P(("grp", "rows"), None, "heads", None),
        P(("grp", "rows")),
        P(("grp", "rows")),
        P(None, ("grp", "rows"), "heads", None),
        P(None, ("grp", "rows"), "heads"),
        P(None, ("grp", "rows"), "heads"),
        P(None, ("grp", "rows")),
        P(None, "heads", None),
        P("heads", None),
        P("heads"),
        P("heads"),
        P("heads"),
        P("heads"),
    )
    out_specs = (
        P(None, ("grp", "rows"), "heads"),
        P(("grp", "rows"), "heads", None, None),
        P(("grp", "rows"), None, "heads", None),
    )
    return jax.shard_map(
        per_device, mesh=mesh, in_specs=in_specs, out_specs=out_specs, check_vma=False
    )
```
